32 devices in a mesh: dp: 4 (over y, x), fsdp: 8 (over z, core).
Axes of the slice: x: 2, y: 2, z: 4, core: 2. Of those that a mesh axis runs over, the one named last changes fastest.
Arguments:
- patches: bfloat16 [1536, 6144], P('dp', 'fsdp'), may hold values from -6 to 6
- gain: float32 [6144], replicated, may hold values from 0.1 to 1.9
- w_up: bfloat16 [6144, 12288], P(None, 'fsdp'), may hold values from -0.109375 to 0.109375
- bias: float32 [12288], P('fsdp'), may hold values from -3 to 3
- grad_hidden: bfloat16 [512, 12288], P('dp', 'fsdp'), may hold values from -6 to 6
- patch_counts: int32 [4, 8], replicated, may hold values from 1 to 48, 128 in all within a row
- image_source: int32 [32], replicated, may hold values from 0 to 31, each once
Outputs:
- hidden: bfloat16 [512, 12288], P('dp', 'fsdp')
- grad_patches: bfloat16 [1536, 6144], P('dp', 'fsdp')
- grad_weight: bfloat16 [6144, 12288], P('dp', 'fsdp')
- grad_bias: float32 [12288], P('fsdp')
- gain_gradient: float32 [6144], P('fsdp')
The draws below stay inside these ranges and needn't reach their ends.
Inputs may be any that keep to these rules, and one draw needn't show every extreme that they name: Each row of patch_counts sums to exactly 128 and has largest entry exactly 48. `image_source`: A permutation: each image number g * 8 + k appears in exactly one slot.
All inputs are finite; a program needn't handle non-finite values.
Results may differ from the reference program's by a relative error of at most 0.0069.
Values may be sent and summed in bfloat16 or wider, within the bound.
A program may use at most 128 MiB of HBM per device.

```python
import math
import jax
import jax.numpy as jnp
import numpy as np
from jax import lax

D = 6144
FFW = 12288
TOK_G = 128
IMGS = 8
CAP = 48
ROWS = 512
SLOTS = 32
N_DP = 4


def spiked(result, key, source, target, parts, factor):
    def block_of(dim):
        return (jnp.arange(result.shape[dim]) // (result.shape[dim] // parts)).reshape((-1,) + (1,) * (result.ndim - 1 - dim))

    first = jax.random.permutation(key, parts)[block_of(target)]
    other_side = (block_of(target) + parts // 2) % parts
    return jnp.where((block_of(source) == first) | (block_of(source) == other_side), factor * result, result)


def shard_levels(own_key, extent, split, smallest, largest):
    level, own = 1.0, jax.random.fold_in(own_key, 6)
    for dim, shards_of in split:
        steps = jnp.exp(jax.random.uniform(jax.random.fold_in(own, dim), (shards_of,), jnp.float32, smallest / len(split), largest / len(split)))
        level = level * jnp.repeat(steps, extent[dim] // shards_of).reshape([-1 if axis == dim else 1 for axis in range(len(extent))])
    return level


def length_profile(amount, total, reach, slope):
    loads = [(1 << 20) // math.isqrt(grade ** slope) + 1 for grade in range(2, amount + 1)]
    rest, holding = total - reach - (amount - 1), [1] * (amount - 1)
    while rest > 0:
        candidates = [i for i in range(amount - 1) if holding[i] < reach]
        mass, remaining = sum([loads[i] for i in candidates]), rest
        for i in candidates:
            addition = min(reach - holding[i], max(1, remaining * loads[i] // mass), rest)
            holding[i] = holding[i] + addition
            rest = rest - addition
    return np.array([reach] + holding)


def uneven(key, amount, total, limit, skew):
    if amount == 2:
        one = jax.random.randint(key, (), max(1, total - limit), min(limit, total - 1) + 1)
        return jnp.stack([one, total - one])
    sizes = jnp.asarray(length_profile(amount, total, limit, skew), jnp.int32)
    pairs = (amount - 1) // 2
    source_of, receiver = sizes[1:1 + 2 * pairs:2], sizes[2:2 + 2 * pairs:2]
    slack = jnp.minimum(source_of - 1, limit - receiver)
    passed = jax.random.randint(jax.random.fold_in(key, 1), (pairs,), 0, 1 << 20) % (slack + 1)
    sizes = sizes.at[1:1 + 2 * pairs:2].set(source_of - passed).at[2:2 + 2 * pairs:2].set(receiver + passed)
    return sizes[jax.random.permutation(jax.random.fold_in(key, 2), amount)]


def centred(key, extent, deviation, limit, pieces=(), held_as=jnp.bfloat16):
    level = shard_levels(key, extent, pieces, -0.22, 0.18) if pieces else 1.0
    drawn = jax.random.normal(key, extent, jnp.float32) * deviation * level
    return jnp.minimum(jnp.maximum(drawn, -limit), limit).astype(held_as)


def heavy_noise(own_key, shape, width, bound, cuts, heavy, held_as=jnp.bfloat16):
    values = width * jax.random.normal(own_key, shape, jnp.float32)
    if cuts:
        values = values * shard_levels(own_key, shape, cuts, -0.22, 0.18)
    return jnp.clip(spiked(values, jax.random.fold_in(own_key, 3), *heavy), -bound, bound).astype(held_as)


def setup_inputs(seed: int = 0) -> dict:
    key_of = jax.random.split(jax.random.key(seed), 8)
    return {
        "patches": centred(key_of[0], (SLOTS * CAP, D), 1.0, 6.0, ((0, 4), (1, 8))),
        "gain": jnp.clip(1.0 + 0.18 * jax.random.normal(key_of[1], (D,), jnp.float32), 0.1, 1.9),
        "w_up": heavy_noise(key_of[2], (D, FFW), D ** -0.5, 0.109375, ((1, 8),), (1, 0, 8, 2.0)),
        "bias": centred(key_of[3], (FFW,), 0.5, 3.0, ((0, 8),), jnp.float32),
        "grad_hidden": centred(key_of[4], (ROWS, FFW), 1.0, 6.0, ((0, 4), (1, 8))),
        "patch_counts": jax.vmap(lambda own: uneven(own, IMGS, TOK_G, CAP, 2))(jax.random.split(key_of[5], N_DP)).reshape((N_DP, IMGS)).astype(jnp.int32),
        "image_source": jax.random.permutation(key_of[6], SLOTS).astype(jnp.int32),
    }


EPS = 1e-06
ROOT_HALF = 0.7071067811865476
INV_ROOT_TAU = 0.3989422804014327

def gelu_parts(preact):
    normal_cdf = 0.5 * (1.0 + lax.erf(preact * ROOT_HALF))
    density = jnp.exp(-0.5 * preact * preact) * INV_ROOT_TAU
    return (preact * normal_cdf, normal_cdf + preact * density)

def layout(patch_counts, image_source, group_rows, capacity):
    groups, images = patch_counts.shape
    total_images = groups * images
    lengths = patch_counts.reshape(total_images).astype(jnp.int32)
    end_rows = jnp.cumsum(patch_counts, axis=1).astype(jnp.int32)
    starts = (end_rows - patch_counts).reshape(total_images).astype(jnp.int32)
    numbers = jnp.arange(total_images, dtype=jnp.int32)
    slot_of = lax.optimization_barrier(jnp.sum(jnp.where(image_source[None, :] == numbers[:, None], numbers[None, :], 0), axis=1)).astype(jnp.int32)
    row_ids = jnp.arange(group_rows, dtype=jnp.int32)
    position = lax.optimization_barrier(jnp.sum((row_ids[None, :, None] >= end_rows[:, None, :]).astype(jnp.int32), axis=2)).astype(jnp.int32)
    image_ids = (jnp.arange(groups, dtype=jnp.int32)[:, None] * images + position).astype(jnp.int32)
    slot_ids = slot_of[image_ids]
    source_row = (slot_ids * capacity + row_ids[None, :] - starts[image_ids]).astype(jnp.int32)
    return (lengths, starts, slot_ids, source_row)

def reference(patches, gain, w_up, bias, grad_hidden, patch_counts, image_source):
    lengths, starts, slot_ids, source_row = layout(patch_counts, image_source, TOK_G, CAP)
    packed = patches[source_row.reshape(-1)]
    values = packed.astype(jnp.float32)
    row_mean = lax.optimization_barrier(jnp.mean(values, axis=1, keepdims=True))
    centred_input = values - row_mean
    variance = lax.optimization_barrier(jnp.mean(centred_input * centred_input, axis=1, keepdims=True))
    inverse_deviation = lax.rsqrt(variance + EPS)
    normalized_input = centred_input * inverse_deviation
    normed_input = (normalized_input * gain).astype(jnp.bfloat16)
    preact = jnp.dot(normed_input, w_up, preferred_element_type=jnp.float32) + bias
    gelu_value, gelu_slope = gelu_parts(preact)
    hidden = gelu_value.astype(jnp.bfloat16)
    feature_gradient = grad_hidden.astype(jnp.float32) * gelu_slope
    grad_pre = feature_gradient.astype(jnp.bfloat16)
    normed_gradient = lax.dot_general(grad_pre, w_up, (((1,), (1,)), ((), ())), preferred_element_type=jnp.float32)
    scaled_input = normed_gradient * gain
    packed_gradient = (inverse_deviation * (scaled_input - lax.optimization_barrier(jnp.mean(scaled_input, axis=1, keepdims=True)) - normalized_input * lax.optimization_barrier(jnp.mean(scaled_input * normalized_input, axis=1, keepdims=True)))).astype(jnp.bfloat16)
    offsets = jnp.arange(CAP, dtype=jnp.int32)
    counts = lengths[image_source]
    usable = offsets[None, :] < counts[:, None]
    rows_at = ((image_source // IMGS)[:, None] * TOK_G + starts[image_source][:, None] + jnp.minimum(offsets[None, :], counts[:, None] - 1)).astype(jnp.int32)
    grad_patches = jnp.where(usable.reshape(-1)[:, None], packed_gradient[rows_at.reshape(-1)], 0).astype(jnp.bfloat16)

    def add_group(running, group):
        rows_u = lax.dynamic_slice_in_dim(normed_input, group * TOK_G, TOK_G, 0)
        rows_g = lax.dynamic_slice_in_dim(grad_pre, group * TOK_G, TOK_G, 0)
        partial_term = lax.dot_general(rows_u, rows_g, (((0,), (0,)), ((), ())), preferred_element_type=jnp.float32).astype(jnp.bfloat16)
        return (running + lax.optimization_barrier(partial_term).astype(jnp.float32), None)
    grad_weight, _ = lax.scan(add_group, jnp.zeros((D, FFW), jnp.float32), jnp.arange(N_DP, dtype=jnp.int32))
    grad_bias = lax.optimization_barrier(jnp.sum(feature_gradient, axis=0))
    gain_gradient = lax.optimization_barrier(jnp.sum(normed_gradient * normalized_input, axis=0))
    return (hidden, grad_patches, grad_weight.astype(jnp.bfloat16), grad_bias, gain_gradient)
```

```python
import jax
import jax.numpy as jnp
from jax import lax
from jax.sharding import PartitionSpec as P

EPS = 1e-06
ROOT_HALF = 0.7071067811865476
INV_ROOT_TAU = 0.3989422804014327


def gelu_parts(preact):
    normal_cdf = 0.5 * (1.0 + lax.erf(preact * ROOT_HALF))
    density = jnp.exp(-0.5 * preact * preact) * INV_ROOT_TAU
    return (preact * normal_cdf, normal_cdf + preact * density)


def destination_rows(patch_counts, image_source, group_index, group_rows, capacity):
    groups, images = patch_counts.shape
    total_images = groups * images
    starts = (jnp.cumsum(patch_counts, axis=1) - patch_counts).reshape(total_images)
    lengths = patch_counts.reshape(total_images)
    mine = lax.dynamic_slice_in_dim(image_source, group_index * images, images, 0)
    chosen = mine[:, None] == jnp.arange(total_images, dtype=jnp.int32)[None, :]
    start = jnp.sum(jnp.where(chosen, starts[None, :], 0), axis=1)
    count = jnp.sum(jnp.where(chosen, lengths[None, :], 0), axis=1)
    offsets = jnp.arange(capacity, dtype=jnp.int32)
    first = (mine // images) * group_rows + start
    rows = jnp.where(offsets[None, :] < count[:, None], first[:, None] + offsets[None, :], -1)
    return rows.reshape(images * capacity)


def split_in_two(values):
    high = values.astype(jnp.bfloat16)
    low = (values - high.astype(jnp.float32)).astype(jnp.bfloat16)
    return high, low


def middle(outgoing, gain, w_up, bias, grad_hidden):
    groups, group_rows, local_width = outgoing.shape
    shards_of = lax.axis_size("fsdp")
    arrived = lax.all_to_all(outgoing, "dp", split_axis=0, concat_axis=0, tiled=True)
    packed = jnp.sum(arrived.astype(jnp.float32), axis=0).astype(jnp.bfloat16)
    gathered = lax.all_gather(packed, "fsdp", axis=1, tiled=True)
    full_width = gathered.shape[1]
    values = gathered.astype(jnp.float32)
    row_mean = jnp.mean(values, axis=1, keepdims=True)
    centred_input = values - row_mean
    variance = jnp.mean(centred_input * centred_input, axis=1)
    inverse_deviation = lax.rsqrt(variance + EPS)
    normalized_input = centred_input * inverse_deviation[:, None]
    normed_input = (normalized_input * gain).astype(jnp.bfloat16)
    preact = jnp.dot(normed_input, w_up, preferred_element_type=jnp.float32) + bias
    gelu_value, gelu_slope = gelu_parts(preact)
    hidden = gelu_value.astype(jnp.bfloat16)
    feature_gradient = grad_hidden.astype(jnp.float32) * gelu_slope
    grad_pre = feature_gradient.astype(jnp.bfloat16)
    piece = lax.all_gather(grad_pre, "dp", axis=0, tiled=True)
    column_rows = lax.all_to_all(normed_input, "dp", split_axis=1, concat_axis=0, tiled=True)
    partial = lax.dot_general(
        w_up, grad_pre, (((1,), (1,)), ((), ())), preferred_element_type=jnp.float32
    )
    scaled_partial = partial * gain[:, None]
    sums = jnp.stack(
        [jnp.sum(scaled_partial, axis=0), jnp.sum(scaled_partial * normalized_input.T, axis=0)]
    )
    high, low = split_in_two(sums)
    extra = jnp.concatenate([high, low, jnp.zeros((12, group_rows), jnp.bfloat16)])
    sent = jnp.concatenate(
        [
            partial.astype(jnp.bfloat16).reshape(shards_of, local_width, group_rows),
            jnp.broadcast_to(extra[None], (shards_of,) + extra.shape),
        ],
        axis=1,
    )
    parts = lax.all_to_all(sent, "fsdp", split_axis=0, concat_axis=0, tiled=True)
    total = jnp.sum(parts.astype(jnp.float32), axis=0)
    normed_gradient = total[:local_width]
    row_sums = total[local_width : local_width + 2] + total[local_width + 2 : local_width + 4]
    feature_offset = lax.axis_index("fsdp") * local_width
    own_input = lax.dynamic_slice_in_dim(gathered, feature_offset, local_width, 1)
    normalized_local = (
        (own_input.astype(jnp.float32) - row_mean) * inverse_deviation[:, None]
    ).T
    gain_mine = lax.dynamic_slice_in_dim(gain, feature_offset, local_width, 0)
    packed_gradient = (
        inverse_deviation[None, :]
        * (
            gain_mine[:, None] * normed_gradient
            - row_sums[0][None, :] / full_width
            - normalized_local * row_sums[1][None, :] / full_width
        )
    ).T.astype(jnp.bfloat16)
    high, low = split_in_two(jnp.sum(normed_gradient * normalized_local, axis=1))
    back = jnp.concatenate(
        [packed_gradient, high[None], low[None], jnp.zeros((14, local_width), jnp.bfloat16)]
    )
    all_back = lax.all_gather(back, "dp", axis=0)
    gain_gradient = jnp.sum(
        all_back[:, group_rows : group_rows + 2].astype(jnp.float32), axis=(0, 1)
    )
    gradients = all_back[:, :group_rows].reshape(groups * group_rows, local_width)
    return hidden, column_rows, piece, gradients, gain_gradient


def shards(patches, gain, w_up, bias, grad_hidden, patch_counts, image_source):
    groups, images = patch_counts.shape
    group_rows = grad_hidden.shape[0]
    capacity = patches.shape[0] // images
    local_width = patches.shape[1]
    rows = destination_rows(
        patch_counts, image_source, lax.axis_index("dp"), group_rows, capacity
    )
    numbers = jnp.arange(groups * group_rows, dtype=jnp.int32)
    placed = (rows[None, :] == numbers[:, None]).astype(jnp.bfloat16)
    outgoing = jnp.dot(placed, patches, preferred_element_type=jnp.float32)
    outgoing = outgoing.astype(jnp.bfloat16).reshape(groups, group_rows, local_width)
    hidden, column_rows, piece, gradients, gain_gradient = middle(
        outgoing, gain, w_up, bias, grad_hidden
    )
    grad_weight = lax.dot_general(
        column_rows, piece, (((0,), (0,)), ((), ())), preferred_element_type=jnp.float32
    ).astype(jnp.bfloat16)
    grad_bias = jnp.sum(piece.astype(jnp.float32), axis=0)
    grad_patches = lax.dot_general(
        placed, gradients, (((0,), (0,)), ((), ())), preferred_element_type=jnp.float32
    ).astype(jnp.bfloat16)
    return (hidden, grad_patches, grad_weight, grad_bias, gain_gradient)


def solution(mesh):
    return jax.shard_map(
        shards,
        mesh=mesh,
        in_specs=(P("dp", "fsdp"), P(), P(None, "fsdp"), P("fsdp"), P("dp", "fsdp"), P(), P()),
        out_specs=(P("dp", "fsdp"), P("dp", "fsdp"), P("dp", "fsdp"), P("fsdp"), P("fsdp")),
        check_vma=False,
    )
```

```python
import functools

import jax
import jax.numpy as jnp
from jax import lax
from jax.experimental import pallas as pl
from jax.experimental.pallas import tpu as pltpu
from jax.sharding import PartitionSpec as P

EPS = 1e-06
ROOT_HALF = 0.7071067811865476
INV_ROOT_TAU = 0.3989422804014327


def gelu_parts(preact):
    normal_cdf = 0.5 * (1.0 + lax.erf(preact * ROOT_HALF))
    density = jnp.exp(-0.5 * preact * preact) * INV_ROOT_TAU
    return (preact * normal_cdf, normal_cdf + preact * density)


def destination_rows(patch_counts, image_source, group_index, group_rows, capacity):
    groups, images = patch_counts.shape
    total_images = groups * images
    starts = (jnp.cumsum(patch_counts, axis=1) - patch_counts).reshape(total_images)
    lengths = patch_counts.reshape(total_images)
    mine = lax.dynamic_slice_in_dim(image_source, group_index * images, images, 0)
    chosen = mine[:, None] == jnp.arange(total_images, dtype=jnp.int32)[None, :]
    start = jnp.sum(jnp.where(chosen, starts[None, :], 0), axis=1)
    count = jnp.sum(jnp.where(chosen, lengths[None, :], 0), axis=1)
    offsets = jnp.arange(capacity, dtype=jnp.int32)
    first = (mine // images) * group_rows + start
    rows = jnp.where(offsets[None, :] < count[:, None], first[:, None] + offsets[None, :], -1)
    return rows.reshape(images * capacity)


def split_in_two(values):
    high = values.astype(jnp.bfloat16)
    low = (values - high.astype(jnp.float32)).astype(jnp.bfloat16)
    return high, low


def middle(outgoing, gain, w_up, bias, grad_hidden):
    groups, group_rows, local_width = outgoing.shape
    shards_of = lax.axis_size("fsdp")
    arrived = lax.all_to_all(outgoing, "dp", split_axis=0, concat_axis=0, tiled=True)
    packed = jnp.sum(arrived.astype(jnp.float32), axis=0).astype(jnp.bfloat16)
    gathered = lax.all_gather(packed, "fsdp", axis=1, tiled=True)
    full_width = gathered.shape[1]
    values = gathered.astype(jnp.float32)
    row_mean = jnp.mean(values, axis=1, keepdims=True)
    centred_input = values - row_mean
    variance = jnp.mean(centred_input * centred_input, axis=1)
    inverse_deviation = lax.rsqrt(variance + EPS)
    normalized_input = centred_input * inverse_deviation[:, None]
    normed_input = (normalized_input * gain).astype(jnp.bfloat16)
    preact = jnp.dot(normed_input, w_up, preferred_element_type=jnp.float32) + bias
    gelu_value, gelu_slope = gelu_parts(preact)
    hidden = gelu_value.astype(jnp.bfloat16)
    feature_gradient = grad_hidden.astype(jnp.float32) * gelu_slope
    grad_pre = feature_gradient.astype(jnp.bfloat16)
    piece = lax.all_gather(grad_pre, "dp", axis=0, tiled=True)
    column_rows = lax.all_to_all(normed_input, "dp", split_axis=1, concat_axis=0, tiled=True)
    partial = lax.dot_general(
        w_up, grad_pre, (((1,), (1,)), ((), ())), preferred_element_type=jnp.float32
    )
    scaled_partial = partial * gain[:, None]
    sums = jnp.stack(
        [jnp.sum(scaled_partial, axis=0), jnp.sum(scaled_partial * normalized_input.T, axis=0)]
    )
    high, low = split_in_two(sums)
    extra = jnp.concatenate([high, low, jnp.zeros((12, group_rows), jnp.bfloat16)])
    sent = jnp.concatenate(
        [
            partial.astype(jnp.bfloat16).reshape(shards_of, local_width, group_rows),
            jnp.broadcast_to(extra[None], (shards_of,) + extra.shape),
        ],
        axis=1,
    )
    parts = lax.all_to_all(sent, "fsdp", split_axis=0, concat_axis=0, tiled=True)
    total = jnp.sum(parts.astype(jnp.float32), axis=0)
    normed_gradient = total[:local_width]
    row_sums = total[local_width : local_width + 2] + total[local_width + 2 : local_width + 4]
    feature_offset = lax.axis_index("fsdp") * local_width
    own_input = lax.dynamic_slice_in_dim(gathered, feature_offset, local_width, 1)
    normalized_local = (
        (own_input.astype(jnp.float32) - row_mean) * inverse_deviation[:, None]
    ).T
    gain_mine = lax.dynamic_slice_in_dim(gain, feature_offset, local_width, 0)
    packed_gradient = (
        inverse_deviation[None, :]
        * (
            gain_mine[:, None] * normed_gradient
            - row_sums[0][None, :] / full_width
            - normalized_local * row_sums[1][None, :] / full_width
        )
    ).T.astype(jnp.bfloat16)
    high, low = split_in_two(jnp.sum(normed_gradient * normalized_local, axis=1))
    back = jnp.concatenate(
        [packed_gradient, high[None], low[None], jnp.zeros((14, local_width), jnp.bfloat16)]
    )
    all_back = lax.all_gather(back, "dp", axis=0)
    gain_gradient = jnp.sum(
        all_back[:, group_rows : group_rows + 2].astype(jnp.float32), axis=(0, 1)
    )
    gradients = all_back[:, :group_rows].reshape(groups * group_rows, local_width)
    return hidden, column_rows, piece, gradients, gain_gradient


def fused_kernel(
    groups, shards_of, outgoing, gain, bias, grad_hidden, w_hbm,
    hidden, columns, pieces, back, gain_sums,
    w_up, arrived, gathered, normed, sib_send, sib_recv, own, sum_send, sum_recv, stats,
    send_sem, recv_sem, load_sem,
):
    group, shard = lax.axis_index("dp"), lax.axis_index("fsdp")
    chip, core = shard // 2, lax.rem(shard, 2)
    chips = shards_of // 2
    sibling = shard + 1 - 2 * core
    rows, width = outgoing.shape[1:]
    full_width = shards_of * width
    hidden_units = bias.shape[1]
    counter = [0]
    pending = []

    def send(source, target, device):
        index = counter[0]
        counter[0] += 1
        copy = pltpu.make_async_remote_copy(
            src_ref=source,
            dst_ref=target,
            send_sem=send_sem.at[index],
            recv_sem=recv_sem.at[index],
            device_id=device,
            device_id_type=pl.DeviceIdType.MESH,
        )
        copy.start()
        pending.append(copy)
        return copy

    def other_group(step):
        return lax.rem(group + step, groups)

    def source_group(step):
        return lax.rem(group - step + groups, groups)

    load = pltpu.make_async_copy(w_hbm, w_up, load_sem)
    load.start()
    barrier = pltpu.get_barrier_semaphore()
    for step in range(1, groups):
        pl.semaphore_signal(barrier, inc=1, device_id={"dp": other_group(step)}, device_id_type=pl.DeviceIdType.MESH)
    for step in range(1, shards_of):
        pl.semaphore_signal(barrier, inc=1, device_id={"fsdp": lax.rem(shard + step, shards_of)}, device_id_type=pl.DeviceIdType.MESH)
    pl.semaphore_wait(barrier, groups + shards_of - 2)

    copies = [
        send(outgoing.at[other_group(step)], arrived.at[step - 1], {"dp": other_group(step)})
        for step in range(1, groups)
    ]
    packed = outgoing[group].astype(jnp.float32)
    for step in range(1, groups):
        copies[step - 1].wait_recv()
        packed = packed + arrived[step - 1].astype(jnp.float32)
    gathered[shard] = packed.astype(jnp.bfloat16)

    copies = [
        send(gathered.at[shard], gathered.at[shard], {"fsdp": lax.rem(chip + step, chips) * 2 + core})
        for step in range(1, chips)
    ]
    forwards = [send(gathered.at[shard], gathered.at[shard], {"fsdp": sibling})]
    for step in range(1, chips):
        copies[step - 1].wait_recv()
        came = lax.rem(chip - step + chips, chips) * 2 + core
        forwards.append(send(gathered.at[came], gathered.at[came], {"fsdp": sibling}))
    for copy in forwards:
        copy.wait_recv()

    total = jnp.zeros((rows, 1), jnp.float32)
    for j in range(shards_of):
        total = total + jnp.sum(gathered[j].astype(jnp.float32), axis=1, keepdims=True)
    mean = total / full_width
    total = jnp.zeros((rows, 1), jnp.float32)
    for j in range(shards_of):
        centred = gathered[j].astype(jnp.float32) - mean
        total = total + jnp.sum(centred * centred, axis=1, keepdims=True)
    inverse = lax.rsqrt(total / full_width + EPS)

    def normalized(j):
        return (gathered[j].astype(jnp.float32) - mean) * inverse

    for j in range(shards_of):
        normed[j] = (normalized(j) * gain[j]).astype(jnp.bfloat16)

    half = pl.ds(pl.multiple_of(core * width, 128), width)
    column_copies = [
        send(normed.at[other_group(step) * 2 + core], columns.at[group, :, half], {"dp": other_group(step)})
        for step in range(1, groups)
    ]
    columns[group, :, :width] = normed[2 * group]
    columns[group, :, width:] = normed[2 * group + 1]

    load.wait()

    def forward(n, carry):
        tile = pl.ds(pl.multiple_of(n * 256, 256), 256)
        acc = jnp.zeros((rows, 256), jnp.float32)
        for j in range(shards_of):
            acc = acc + jnp.dot(
                normed[j], w_up[j * width : (j + 1) * width, tile], preferred_element_type=jnp.float32
            )
        value, slope = gelu_parts(acc + bias[:, tile])
        hidden[:, tile] = value.astype(jnp.bfloat16)
        pieces[group, :, tile] = (grad_hidden[:, tile].astype(jnp.float32) * slope).astype(jnp.bfloat16)
        return carry

    lax.fori_loop(0, hidden_units // 256, forward, 0)
    piece_copies = [
        send(pieces.at[group], pieces.at[group], {"dp": other_group(step)}) for step in range(1, groups)
    ]

    def partial(j):
        lanes = pl.ds(pl.multiple_of(j * width, 128), width)
        return lax.dot_general(
            pieces[group], w_up[lanes, :], (((1,), (1,)), ((), ())), preferred_element_type=jnp.float32
        )

    plain = jnp.zeros((rows, 1), jnp.float32)
    weighted = jnp.zeros((rows, 1), jnp.float32)
    sib_copies, sum_copies = [], []

    def pass_on(i):
        sib_copies[i].wait_recv()
        sum_send[i] = (own[i] + sib_recv[i].astype(jnp.float32)).astype(jnp.bfloat16)
        target = lax.rem(chip + 1 + i, chips) * 2 + core
        sum_copies.append(send(sum_send.at[i], sum_recv.at[i], {"fsdp": target}))

    for i in range(chips):
        base = lax.rem(chip + 1 + i, chips) * 2
        for mine in (False, True):
            j = base + (core if mine else 1 - core)
            part = partial(j)
            scaled = part * gain[j]
            plain = plain + jnp.sum(scaled, axis=1, keepdims=True)
            weighted = weighted + jnp.sum(scaled * normalized(j), axis=1, keepdims=True)
            if mine:
                own[i] = part
            else:
                sib_send[i] = part.astype(jnp.bfloat16)
                sib_copies.append(send(sib_send.at[i], sib_recv.at[i], {"fsdp": sibling}))
        if i > 0:
            pass_on(i - 1)

    lane = lax.broadcasted_iota(jnp.int32, (rows, rows), 1)
    both = jnp.where(lane == 0, plain, jnp.where(lane == 1, weighted, 0.0))
    stats[shard] = both.T[:8]
    stat_copies = [
        send(stats.at[shard], stats.at[shard], {"fsdp": lax.rem(shard + step, shards_of)})
        for step in range(1, shards_of)
    ]
    for step in range(1, groups):
        column_copies[step - 1].wait_recv()
        came = columns.at[source_group(step), :, half]
        column_copies.append(send(came, came, {"fsdp": sibling}))

    for copy in stat_copies:
        copy.wait_recv()
    summed = stats[0]
    for j in range(1, shards_of):
        summed = summed + stats[j]
    upright = jnp.concatenate([summed, jnp.zeros((rows - 8, rows), jnp.float32)], axis=0).T
    plain_mean = upright[:, 0:1] / full_width
    weighted_mean = upright[:, 1:2] / full_width
    sib_copies[chips - 1].wait_recv()
    gradient = own[chips - 1] + sib_recv[chips - 1].astype(jnp.float32)
    for i in range(chips - 1):
        sum_copies[i].wait_recv()
        gradient = gradient + sum_recv[i].astype(jnp.float32)
    local = normalized(shard)
    back[group] = (
        inverse * (gradient * gain[shard] - plain_mean - local * weighted_mean)
    ).astype(jnp.bfloat16)
    gain_sums[group] = jnp.broadcast_to(jnp.sum(gradient * local, axis=0, keepdims=True), (8, width))
    last = []
    for step in range(1, groups):
        device = {"dp": other_group(step)}
        last.append(send(back.at[group], back.at[group], device))
        last.append(send(gain_sums.at[group], gain_sums.at[group], device))
    for copy in column_copies[groups - 1 :] + piece_copies + last:
        copy.wait_recv()
    for copy in pending:
        copy.wait_send()


def fused(outgoing, gain, w_up, bias, grad_hidden):
    groups, rows, width = outgoing.shape
    shards_of = lax.axis_size("fsdp")
    hidden_units = bias.shape[0]
    chips = shards_of // 2
    bf16, f32 = jnp.bfloat16, jnp.float32
    copies = 4 * (groups - 1) + 2 * (groups - 1) + 2 * (chips - 1) + 2 * chips + shards_of - 1
    vmem = pl.BlockSpec(memory_space=pltpu.VMEM)
    hidden, columns, pieces, back, gain_sums = pl.pallas_call(
        functools.partial(fused_kernel, groups, shards_of),
        out_shape=[
            jax.ShapeDtypeStruct((rows, hidden_units), bf16),
            jax.ShapeDtypeStruct((groups, rows, 2 * width), bf16),
            jax.ShapeDtypeStruct((groups, rows, hidden_units), bf16),
            jax.ShapeDtypeStruct((groups, rows, width), bf16),
            jax.ShapeDtypeStruct((groups, 8, width), f32),
        ],
        in_specs=[vmem] * 4 + [pl.BlockSpec(memory_space=pl.ANY)],
        out_specs=[vmem] * 5,
        scratch_shapes=[
            pltpu.VMEM(w_up.shape, bf16),
            pltpu.VMEM((groups - 1, rows, width), bf16),
            pltpu.VMEM((shards_of, rows, width), bf16),
            pltpu.VMEM((shards_of, rows, width), bf16),
            pltpu.VMEM((chips, rows, width), bf16),
            pltpu.VMEM((chips, rows, width), bf16),
            pltpu.VMEM((chips, rows, width), f32),
            pltpu.VMEM((chips - 1, rows, width), bf16),
            pltpu.VMEM((chips - 1, rows, width), bf16),
            pltpu.VMEM((shards_of, 8, rows), f32),
            pltpu.SemaphoreType.DMA((copies,)),
            pltpu.SemaphoreType.DMA((copies,)),
            pltpu.SemaphoreType.DMA,
        ],
        compiler_params=pltpu.CompilerParams(
            collective_id=0, has_side_effects=True, vmem_limit_bytes=50 * 1024 * 1024
        ),
    )(outgoing, gain.reshape(shards_of, 1, width), bias[None], grad_hidden, w_up)
    return (
        hidden,
        columns.reshape(groups * rows, 2 * width),
        pieces.reshape(groups * rows, hidden_units),
        back.reshape(groups * rows, width),
        jnp.sum(gain_sums[:, 0], axis=0),
    )


def fits_tiles(groups, shards_of, rows, width, hidden_units):
    return (
        shards_of == 2 * groups and rows == 128 and width % 128 == 0 and hidden_units % 256 == 0
    )


def shards(patches, gain, w_up, bias, grad_hidden, patch_counts, image_source):
    groups, images = patch_counts.shape
    group_rows = grad_hidden.shape[0]
    capacity = patches.shape[0] // images
    local_width = patches.shape[1]
    rows = destination_rows(
        patch_counts, image_source, lax.axis_index("dp"), group_rows, capacity
    )
    numbers = jnp.arange(groups * group_rows, dtype=jnp.int32)
    placed = (rows[None, :] == numbers[:, None]).astype(jnp.bfloat16)
    outgoing = jnp.dot(placed, patches, preferred_element_type=jnp.float32)
    outgoing = outgoing.astype(jnp.bfloat16).reshape(groups, group_rows, local_width)
    tiled = fits_tiles(
        groups, lax.axis_size("fsdp"), group_rows, local_width, grad_hidden.shape[1]
    )
    arrange = fused if tiled else middle
    hidden, column_rows, piece, gradients, gain_gradient = arrange(
        outgoing, gain, w_up, bias, grad_hidden
    )
    grad_weight = lax.dot_general(
        column_rows, piece, (((0,), (0,)), ((), ())), preferred_element_type=jnp.float32
    ).astype(jnp.bfloat16)
    grad_bias = jnp.sum(piece.astype(jnp.float32), axis=0)
    grad_patches = lax.dot_general(
        placed, gradients, (((0,), (0,)), ((), ())), preferred_element_type=jnp.float32
    ).astype(jnp.bfloat16)
    return (hidden, grad_patches, grad_weight, grad_bias, gain_gradient)


def solution(mesh):
    return jax.shard_map(
        shards,
        mesh=mesh,
        in_specs=(P("dp", "fsdp"), P(), P(None, "fsdp"), P("fsdp"), P("dp", "fsdp"), P(), P()),
        out_specs=(P("dp", "fsdp"), P("dp", "fsdp"), P("dp", "fsdp"), P("fsdp"), P("fsdp")),
        check_vma=False,
    )
```

```python
import functools

import jax
import jax.numpy as jnp
from jax import lax
from jax.experimental import pallas as pl
from jax.experimental.pallas import tpu as pltpu
from jax.sharding import PartitionSpec as P

EPS = 1e-06
PARTS = 4
ROOT_HALF = 0.7071067811865476
INV_ROOT_TAU = 0.3989422804014327


def gelu_parts(preact):
    normal_cdf = 0.5 * (1.0 + lax.erf(preact * ROOT_HALF))
    density = jnp.exp(-0.5 * preact * preact) * INV_ROOT_TAU
    return (preact * normal_cdf, normal_cdf + preact * density)


def destination_rows(patch_counts, image_source, group_index, group_rows, capacity):
    groups, images = patch_counts.shape
    numbers = jnp.arange(groups * images, dtype=jnp.int32)[None, :]
    lengths = patch_counts.reshape(1, groups * images)
    mine = lax.dynamic_slice_in_dim(image_source, group_index * images, images, 0)
    image = mine[:, None]
    before = (numbers // images == image // images) & (numbers < image)
    start = jnp.sum(jnp.where(before, lengths, 0), axis=1)
    count = jnp.sum(jnp.where(numbers == image, lengths, 0), axis=1)
    offsets = jnp.arange(capacity, dtype=jnp.int32)
    first = (mine // images) * group_rows + start
    rows = jnp.where(offsets[None, :] < count[:, None], first[:, None] + offsets[None, :], -1)
    return rows.reshape(images * capacity)


def split_in_two(values):
    high = values.astype(jnp.bfloat16)
    low = (values - high.astype(jnp.float32)).astype(jnp.bfloat16)
    return high, low


def middle(outgoing, gain, w_up, bias, grad_hidden):
    groups, group_rows, local_width = outgoing.shape
    shards_of = lax.axis_size("fsdp")
    arrived = lax.all_to_all(outgoing, "dp", split_axis=0, concat_axis=0, tiled=True)
    packed = jnp.sum(arrived.astype(jnp.float32), axis=0).astype(jnp.bfloat16)
    gathered = lax.all_gather(packed, "fsdp", axis=1, tiled=True)
    full_width = gathered.shape[1]
    values = gathered.astype(jnp.float32)
    row_mean = jnp.mean(values, axis=1, keepdims=True)
    centred_input = values - row_mean
    variance = jnp.mean(centred_input * centred_input, axis=1)
    inverse_deviation = lax.rsqrt(variance + EPS)
    normalized_input = centred_input * inverse_deviation[:, None]
    normed_input = (normalized_input * gain).astype(jnp.bfloat16)
    preact = jnp.dot(normed_input, w_up, preferred_element_type=jnp.float32) + bias
    gelu_value, gelu_slope = gelu_parts(preact)
    hidden = gelu_value.astype(jnp.bfloat16)
    feature_gradient = grad_hidden.astype(jnp.float32) * gelu_slope
    grad_pre = feature_gradient.astype(jnp.bfloat16)
    piece = lax.all_gather(grad_pre, "dp", axis=0, tiled=True)
    column_rows = lax.all_to_all(normed_input, "dp", split_axis=1, concat_axis=0, tiled=True)
    partial = lax.dot_general(
        w_up, grad_pre, (((1,), (1,)), ((), ())), preferred_element_type=jnp.float32
    )
    scaled_partial = partial * gain[:, None]
    sums = jnp.stack(
        [jnp.sum(scaled_partial, axis=0), jnp.sum(scaled_partial * normalized_input.T, axis=0)]
    )
    high, low = split_in_two(sums)
    extra = jnp.concatenate([high, low, jnp.zeros((12, group_rows), jnp.bfloat16)])
    sent = jnp.concatenate(
        [
            partial.astype(jnp.bfloat16).reshape(shards_of, local_width, group_rows),
            jnp.broadcast_to(extra[None], (shards_of,) + extra.shape),
        ],
        axis=1,
    )
    parts = lax.all_to_all(sent, "fsdp", split_axis=0, concat_axis=0, tiled=True)
    total = jnp.sum(parts.astype(jnp.float32), axis=0)
    normed_gradient = total[:local_width]
    row_sums = total[local_width : local_width + 2] + total[local_width + 2 : local_width + 4]
    feature_offset = lax.axis_index("fsdp") * local_width
    own_input = lax.dynamic_slice_in_dim(gathered, feature_offset, local_width, 1)
    normalized_local = (
        (own_input.astype(jnp.float32) - row_mean) * inverse_deviation[:, None]
    ).T
    gain_mine = lax.dynamic_slice_in_dim(gain, feature_offset, local_width, 0)
    packed_gradient = (
        inverse_deviation[None, :]
        * (
            gain_mine[:, None] * normed_gradient
            - row_sums[0][None, :] / full_width
            - normalized_local * row_sums[1][None, :] / full_width
        )
    ).T.astype(jnp.bfloat16)
    high, low = split_in_two(jnp.sum(normed_gradient * normalized_local, axis=1))
    back = jnp.concatenate(
        [packed_gradient, high[None], low[None], jnp.zeros((14, local_width), jnp.bfloat16)]
    )
    all_back = lax.all_gather(back, "dp", axis=0)
    gain_gradient = jnp.sum(
        all_back[:, group_rows : group_rows + 2].astype(jnp.float32), axis=(0, 1)
    )
    gradients = all_back[:, :group_rows].reshape(groups * group_rows, local_width)
    return hidden, column_rows, piece, gradients, gain_gradient


def fused_kernel(
    groups, shards_of, outgoing, gain, bias, grad_hidden, w_hbm,
    hidden, columns, pieces, back, gain_sums,
    w_up, arrived, gathered, normed, sib_send, sib_recv, own, sum_send, sum_recv, stats, means, squares,
    send_sem, recv_sem, load_sem,
):
    group, shard = lax.axis_index("dp"), lax.axis_index("fsdp")
    chip, core = shard // 2, lax.rem(shard, 2)
    chips = shards_of // 2
    sibling = shard + 1 - 2 * core
    rows, width = outgoing.shape[1:]
    full_width = shards_of * width
    hidden_units = bias.shape[1]
    counter = [0]
    pending = []

    def send(source, target, device, when=None):
        index = counter[0]
        counter[0] += 1
        copy = pltpu.make_async_remote_copy(
            src_ref=source,
            dst_ref=target,
            send_sem=send_sem.at[index],
            recv_sem=recv_sem.at[index],
            device_id=device,
            device_id_type=pl.DeviceIdType.MESH,
        )
        if when is None:
            copy.start()
        else:
            pl.when(when)(copy.start)
        pending.append((copy, when))
        return copy

    def other_group(step):
        return lax.rem(group + step, groups)

    def source_group(step):
        return lax.rem(group - step + groups, groups)

    load = pltpu.make_async_copy(w_hbm, w_up, load_sem)
    load.start()
    barrier = pltpu.get_barrier_semaphore()
    for step in range(1, groups):
        pl.semaphore_signal(barrier, inc=1, device_id={"dp": other_group(step)}, device_id_type=pl.DeviceIdType.MESH)
    for step in range(1, shards_of):
        pl.semaphore_signal(barrier, inc=1, device_id={"fsdp": lax.rem(shard + step, shards_of)}, device_id_type=pl.DeviceIdType.MESH)
    pl.semaphore_wait(barrier, groups + shards_of - 2)

    depth = rows // PARTS
    spans = [pl.ds(h * depth, depth) for h in range(PARTS)]
    row_copies = [
        [
            send(
                outgoing.at[other_group(step), span],
                arrived.at[step - 1, span],
                {"dp": other_group(step)},
            )
            for step in range(1, groups)
        ]
        for span in spans
    ]

    right_chip = {"fsdp": lax.rem(chip + 1, chips) * 2 + core}
    left_chip = {"fsdp": lax.rem(chip + chips - 1, chips) * 2 + core}
    beside = {"fsdp": sibling}
    has_right, has_left = chip < chips - 1, chip > 0

    def spread(j, span, device, when=None):
        return send(gathered.at[j, span], gathered.at[j, span], device, when)

    def row_statistics(j):
        values = gathered[j].astype(jnp.float32)
        mean = jnp.sum(values, axis=1, keepdims=True) / width
        means[j] = mean
        squares[j] = jnp.sum((values - mean) * (values - mean), axis=1, keepdims=True)

    def other_core(j):
        return j + 1 - 2 * core

    rightward, leftward, own_beside = [], [], []
    for h, span in enumerate(spans):
        packed = outgoing[group, span].astype(jnp.float32)
        for step in range(1, groups):
            row_copies[h][step - 1].wait_recv()
            packed = packed + arrived[step - 1, span].astype(jnp.float32)
        gathered[shard, span] = packed.astype(jnp.bfloat16)
        rightward.append(spread(shard, span, right_chip, has_right))
        leftward.append(spread(shard, span, left_chip, has_left))
        own_beside.append(spread(shard, span, beside))
    row_statistics(shard)
    waiting = [(None, other_core(shard), own_beside)]

    def take_beside(when, j, copies):
        def take():
            for copy in copies:
                copy.wait_recv()
            row_statistics(j)

        if when is None:
            take()
        else:
            pl.when(when)(take)

    for step in range(1, chips):
        streams = [
            (chip >= step, has_right, right_chip, lax.rem(chip - step + chips, chips), rightward),
            (chip + step < chips, has_left, left_chip, lax.rem(chip + step, chips), leftward),
        ]
        besides = [[], []]
        for h, span in enumerate(spans):
            for side, (here, onward, device, came, stream) in enumerate(streams):
                j = came * 2 + core
                pl.when(here)(stream[h].wait_recv)
                if step < chips - 1:
                    stream[h] = spread(j, span, device, jnp.logical_and(here, onward))
                besides[side].append(spread(j, span, beside, here))
        for entry in waiting:
            take_beside(*entry)
        waiting = []
        for side, (here, onward, device, came, stream) in enumerate(streams):
            j = came * 2 + core
            pl.when(here)(functools.partial(row_statistics, j))
            waiting.append((here, other_core(j), besides[side]))
    for entry in waiting:
        take_beside(*entry)

    mean = means[0]
    for j in range(1, shards_of):
        mean = mean + means[j]
    mean = mean / shards_of
    total = jnp.zeros((rows, 1), jnp.float32)
    for j in range(shards_of):
        offset = means[j] - mean
        total = total + squares[j] + width * (offset * offset)
    inverse = lax.rsqrt(total / full_width + EPS)

    def normalized(j):
        return (gathered[j].astype(jnp.float32) - mean) * inverse

    for j in range(shards_of):
        normed[j] = (normalized(j) * gain[j]).astype(jnp.bfloat16)

    half = pl.ds(pl.multiple_of(core * width, 128), width)
    column_copies = [
        send(normed.at[other_group(step) * 2 + core], columns.at[group, :, half], {"dp": other_group(step)})
        for step in range(1, groups)
    ]
    columns[group, :, :width] = normed[2 * group]
    columns[group, :, width:] = normed[2 * group + 1]

    load.wait()

    def forward(n, carry):
        tile = pl.ds(pl.multiple_of(n * 256, 256), 256)
        acc = jnp.zeros((rows, 256), jnp.float32)
        for j in range(shards_of):
            acc = acc + jnp.dot(
                normed[j], w_up[j * width : (j + 1) * width, tile], preferred_element_type=jnp.float32
            )
        value, slope = gelu_parts(acc + bias[:, tile])
        hidden[:, tile] = value.astype(jnp.bfloat16)
        pieces[group, :, tile] = (grad_hidden[:, tile].astype(jnp.float32) * slope).astype(jnp.bfloat16)
        return carry

    lax.fori_loop(0, hidden_units // 256, forward, 0)
    piece_copies = [
        send(pieces.at[group], pieces.at[group], {"dp": other_group(step)}) for step in range(1, groups)
    ]

    def partial(j):
        lanes = pl.ds(pl.multiple_of(j * width, 128), width)
        return lax.dot_general(
            pieces[group], w_up[lanes, :], (((1,), (1,)), ((), ())), preferred_element_type=jnp.float32
        )

    plain = jnp.zeros((rows, 1), jnp.float32)
    weighted = jnp.zeros((rows, 1), jnp.float32)
    sib_copies, sum_copies = [], []

    def pass_on(i):
        sib_copies[i].wait_recv()
        sum_send[i] = (own[i] + sib_recv[i].astype(jnp.float32)).astype(jnp.bfloat16)
        target = lax.rem(chip + 1 + i, chips) * 2 + core
        sum_copies.append(send(sum_send.at[i], sum_recv.at[i], {"fsdp": target}))

    for i in range(chips):
        base = lax.rem(chip + 1 + i, chips) * 2
        for mine in (False, True):
            j = base + (core if mine else 1 - core)
            part = partial(j)
            scaled = part * gain[j]
            plain = plain + jnp.sum(scaled, axis=1, keepdims=True)
            weighted = weighted + jnp.sum(scaled * normalized(j), axis=1, keepdims=True)
            if mine:
                own[i] = part
            else:
                sib_send[i] = part.astype(jnp.bfloat16)
                sib_copies.append(send(sib_send.at[i], sib_recv.at[i], {"fsdp": sibling}))
        if i > 0:
            pass_on(i - 1)

    lane = lax.broadcasted_iota(jnp.int32, (rows, rows), 1)
    both = jnp.where(lane == 0, plain, jnp.where(lane == 1, weighted, 0.0))
    stats[shard] = both.T[:8]
    stat_copies = [
        send(stats.at[shard], stats.at[shard], {"fsdp": lax.rem(shard + step, shards_of)})
        for step in range(1, shards_of)
    ]
    for step in range(1, groups):
        column_copies[step - 1].wait_recv()
        came = columns.at[source_group(step), :, half]
        column_copies.append(send(came, came, {"fsdp": sibling}))

    for copy in stat_copies:
        copy.wait_recv()
    summed = stats[0]
    for j in range(1, shards_of):
        summed = summed + stats[j]
    upright = jnp.concatenate([summed, jnp.zeros((rows - 8, rows), jnp.float32)], axis=0).T
    plain_mean = upright[:, 0:1] / full_width
    weighted_mean = upright[:, 1:2] / full_width
    sib_copies[chips - 1].wait_recv()
    gradient = own[chips - 1] + sib_recv[chips - 1].astype(jnp.float32)
    for i in range(chips - 1):
        sum_copies[i].wait_recv()
        gradient = gradient + sum_recv[i].astype(jnp.float32)
    local = normalized(shard)
    back[group] = (
        inverse * (gradient * gain[shard] - plain_mean - local * weighted_mean)
    ).astype(jnp.bfloat16)
    gain_sums[group] = jnp.broadcast_to(jnp.sum(gradient * local, axis=0, keepdims=True), (8, width))
    last = []
    for step in range(1, groups):
        device = {"dp": other_group(step)}
        last.append(send(back.at[group], back.at[group], device))
        last.append(send(gain_sums.at[group], gain_sums.at[group], device))
    for copy in column_copies[groups - 1 :] + piece_copies + last:
        copy.wait_recv()
    for copy, when in pending:
        if when is None:
            copy.wait_send()
        else:
            pl.when(when)(copy.wait_send)


def fused(outgoing, gain, w_up, bias, grad_hidden):
    groups, rows, width = outgoing.shape
    shards_of = lax.axis_size("fsdp")
    hidden_units = bias.shape[0]
    chips = shards_of // 2
    bf16, f32 = jnp.bfloat16, jnp.float32
    copies = (
        (PARTS + 5) * (groups - 1) + PARTS * (4 * chips - 3) + 2 * chips - 1 + shards_of - 1
    )
    vmem = pl.BlockSpec(memory_space=pltpu.VMEM)
    hidden, columns, pieces, back, gain_sums = pl.pallas_call(
        functools.partial(fused_kernel, groups, shards_of),
        out_shape=[
            jax.ShapeDtypeStruct((rows, hidden_units), bf16),
            jax.ShapeDtypeStruct((groups, rows, 2 * width), bf16),
            jax.ShapeDtypeStruct((groups, rows, hidden_units), bf16),
            jax.ShapeDtypeStruct((groups, rows, width), bf16),
            jax.ShapeDtypeStruct((groups, 8, width), f32),
        ],
        in_specs=[vmem] * 4 + [pl.BlockSpec(memory_space=pl.ANY)],
        out_specs=[vmem] * 5,
        scratch_shapes=[
            pltpu.VMEM(w_up.shape, bf16),
            pltpu.VMEM((groups - 1, rows, width), bf16),
            pltpu.VMEM((shards_of, rows, width), bf16),
            pltpu.VMEM((shards_of, rows, width), bf16),
            pltpu.VMEM((chips, rows, width), bf16),
            pltpu.VMEM((chips, rows, width), bf16),
            pltpu.VMEM((chips, rows, width), f32),
            pltpu.VMEM((chips - 1, rows, width), bf16),
            pltpu.VMEM((chips - 1, rows, width), bf16),
            pltpu.VMEM((shards_of, 8, rows), f32),
            pltpu.VMEM((shards_of, rows, 1), f32),
            pltpu.VMEM((shards_of, rows, 1), f32),
            pltpu.SemaphoreType.DMA((copies,)),
            pltpu.SemaphoreType.DMA((copies,)),
            pltpu.SemaphoreType.DMA,
        ],
        compiler_params=pltpu.CompilerParams(
            collective_id=0, has_side_effects=True, vmem_limit_bytes=50 * 1024 * 1024
        ),
    )(outgoing, gain.reshape(shards_of, 1, width), bias[None], grad_hidden, w_up)
    return (
        hidden,
        columns.reshape(groups * rows, 2 * width),
        pieces.reshape(groups * rows, hidden_units),
        back.reshape(groups * rows, width),
        jnp.sum(gain_sums[:, 0], axis=0),
    )


def fits_tiles(groups, shards_of, rows, width, hidden_units):
    return (
        shards_of == 2 * groups and rows == 128 and width % 128 == 0 and hidden_units % 256 == 0
    )


def shards(patches, gain, w_up, bias, grad_hidden, patch_counts, image_source):
    groups, images = patch_counts.shape
    group_rows = grad_hidden.shape[0]
    capacity = patches.shape[0] // images
    local_width = patches.shape[1]
    rows = destination_rows(
        patch_counts, image_source, lax.axis_index("dp"), group_rows, capacity
    )
    numbers = jnp.arange(groups * group_rows, dtype=jnp.int32)
    placed = (rows[None, :] == numbers[:, None]).astype(jnp.bfloat16)
    outgoing = jnp.dot(placed, patches, preferred_element_type=jnp.float32)
    outgoing = outgoing.astype(jnp.bfloat16).reshape(groups, group_rows, local_width)
    tiled = fits_tiles(
        groups, lax.axis_size("fsdp"), group_rows, local_width, grad_hidden.shape[1]
    )
    arrange = fused if tiled else middle
    hidden, column_rows, piece, gradients, gain_gradient = arrange(
        outgoing, gain, w_up, bias, grad_hidden
    )
    grad_weight = lax.dot_general(
        column_rows, piece, (((0,), (0,)), ((), ())), preferred_element_type=jnp.float32
    ).astype(jnp.bfloat16)
    grad_bias = jnp.sum(piece.astype(jnp.float32), axis=0)
    grad_patches = lax.dot_general(
        placed, gradients, (((0,), (0,)), ((), ())), preferred_element_type=jnp.float32
    ).astype(jnp.bfloat16)
    return (hidden, grad_patches, grad_weight, grad_bias, gain_gradient)


def solution(mesh):
    return jax.shard_map(
        shards,
        mesh=mesh,
        in_specs=(P("dp", "fsdp"), P(), P(None, "fsdp"), P("fsdp"), P("dp", "fsdp"), P(), P()),
        out_specs=(P("dp", "fsdp"), P("dp", "fsdp"), P("dp", "fsdp"), P("fsdp"), P("fsdp")),
        check_vma=False,
    )
```

```python
import functools

import jax
import jax.numpy as jnp
from jax import lax
from jax.experimental import pallas as pl
from jax.experimental.pallas import tpu as pltpu
from jax.sharding import PartitionSpec as P

EPS = 1e-06
PARTS = 4
ROOT_HALF = 0.7071067811865476
INV_ROOT_TAU = 0.3989422804014327


def gelu_parts(preact):
    normal_cdf = 0.5 * (1.0 + lax.erf(preact * ROOT_HALF))
    density = jnp.exp(-0.5 * preact * preact) * INV_ROOT_TAU
    return (preact * normal_cdf, normal_cdf + preact * density)


def destination_rows(patch_counts, image_source, group_index, group_rows, capacity):
    groups, images = patch_counts.shape
    numbers = jnp.arange(groups * images, dtype=jnp.int32)[None, :]
    lengths = patch_counts.reshape(1, groups * images)
    mine = lax.dynamic_slice_in_dim(image_source, group_index * images, images, 0)
    image = mine[:, None]
    before = (numbers // images == image // images) & (numbers < image)
    start = jnp.sum(jnp.where(before, lengths, 0), axis=1)
    count = jnp.sum(jnp.where(numbers == image, lengths, 0), axis=1)
    offsets = jnp.arange(capacity, dtype=jnp.int32)
    first = (mine // images) * group_rows + start
    rows = jnp.where(offsets[None, :] < count[:, None], first[:, None] + offsets[None, :], -1)
    return rows.reshape(images * capacity)


def split_in_two(values):
    high = values.astype(jnp.bfloat16)
    low = (values - high.astype(jnp.float32)).astype(jnp.bfloat16)
    return high, low


def middle(outgoing, gain, w_up, bias, grad_hidden):
    groups, group_rows, local_width = outgoing.shape
    shards_of = lax.axis_size("fsdp")
    arrived = lax.all_to_all(outgoing, "dp", split_axis=0, concat_axis=0, tiled=True)
    packed = jnp.sum(arrived.astype(jnp.float32), axis=0).astype(jnp.bfloat16)
    gathered = lax.all_gather(packed, "fsdp", axis=1, tiled=True)
    full_width = gathered.shape[1]
    values = gathered.astype(jnp.float32)
    row_mean = jnp.mean(values, axis=1, keepdims=True)
    centred_input = values - row_mean
    variance = jnp.mean(centred_input * centred_input, axis=1)
    inverse_deviation = lax.rsqrt(variance + EPS)
    normalized_input = centred_input * inverse_deviation[:, None]
    normed_input = (normalized_input * gain).astype(jnp.bfloat16)
    preact = jnp.dot(normed_input, w_up, preferred_element_type=jnp.float32) + bias
    gelu_value, gelu_slope = gelu_parts(preact)
    hidden = gelu_value.astype(jnp.bfloat16)
    feature_gradient = grad_hidden.astype(jnp.float32) * gelu_slope
    grad_pre = feature_gradient.astype(jnp.bfloat16)
    piece = lax.all_gather(grad_pre, "dp", axis=0, tiled=True)
    column_rows = lax.all_to_all(normed_input, "dp", split_axis=1, concat_axis=0, tiled=True)
    partial = lax.dot_general(
        w_up, grad_pre, (((1,), (1,)), ((), ())), preferred_element_type=jnp.float32
    )
    scaled_partial = partial * gain[:, None]
    sums = jnp.stack(
        [jnp.sum(scaled_partial, axis=0), jnp.sum(scaled_partial * normalized_input.T, axis=0)]
    )
    high, low = split_in_two(sums)
    extra = jnp.concatenate([high, low, jnp.zeros((12, group_rows), jnp.bfloat16)])
    sent = jnp.concatenate(
        [
            partial.astype(jnp.bfloat16).reshape(shards_of, local_width, group_rows),
            jnp.broadcast_to(extra[None], (shards_of,) + extra.shape),
        ],
        axis=1,
    )
    parts = lax.all_to_all(sent, "fsdp", split_axis=0, concat_axis=0, tiled=True)
    total = jnp.sum(parts.astype(jnp.float32), axis=0)
    normed_gradient = total[:local_width]
    row_sums = total[local_width : local_width + 2] + total[local_width + 2 : local_width + 4]
    feature_offset = lax.axis_index("fsdp") * local_width
    own_input = lax.dynamic_slice_in_dim(gathered, feature_offset, local_width, 1)
    normalized_local = (
        (own_input.astype(jnp.float32) - row_mean) * inverse_deviation[:, None]
    ).T
    gain_mine = lax.dynamic_slice_in_dim(gain, feature_offset, local_width, 0)
    packed_gradient = (
        inverse_deviation[None, :]
        * (
            gain_mine[:, None] * normed_gradient
            - row_sums[0][None, :] / full_width
            - normalized_local * row_sums[1][None, :] / full_width
        )
    ).T.astype(jnp.bfloat16)
    high, low = split_in_two(jnp.sum(normed_gradient * normalized_local, axis=1))
    back = jnp.concatenate(
        [packed_gradient, high[None], low[None], jnp.zeros((14, local_width), jnp.bfloat16)]
    )
    all_back = lax.all_gather(back, "dp", axis=0)
    gain_gradient = jnp.sum(
        all_back[:, group_rows : group_rows + 2].astype(jnp.float32), axis=(0, 1)
    )
    gradients = all_back[:, :group_rows].reshape(groups * group_rows, local_width)
    grad_weight = lax.dot_general(
        column_rows, piece, (((0,), (0,)), ((), ())), preferred_element_type=jnp.float32
    ).astype(jnp.bfloat16)
    grad_bias = jnp.sum(piece.astype(jnp.float32), axis=0)
    return hidden, grad_weight, grad_bias, gradients, gain_gradient


def fused_kernel(
    groups, shards_of, outgoing, gain, bias, grad_hidden, w_hbm,
    hidden, grad_weight, grad_bias, back, gain_sums,
    columns, pieces, w_up, arrived, gathered, normed, sib_send, sib_recv, own, sum_send, sum_recv, stats, means, squares,
    send_sem, recv_sem, load_sem,
):
    group, shard = lax.axis_index("dp"), lax.axis_index("fsdp")
    chip, core = shard // 2, lax.rem(shard, 2)
    chips = shards_of // 2
    sibling = shard + 1 - 2 * core
    rows, width = outgoing.shape[1:]
    full_width = shards_of * width
    hidden_units = bias.shape[1]
    counter = [0]
    pending = []

    def send(source, target, device, when=None):
        index = counter[0]
        counter[0] += 1
        copy = pltpu.make_async_remote_copy(
            src_ref=source,
            dst_ref=target,
            send_sem=send_sem.at[index],
            recv_sem=recv_sem.at[index],
            device_id=device,
            device_id_type=pl.DeviceIdType.MESH,
        )
        if when is None:
            copy.start()
        else:
            pl.when(when)(copy.start)
        pending.append((copy, when))
        return copy

    def other_group(step):
        return lax.rem(group + step, groups)

    def source_group(step):
        return lax.rem(group - step + groups, groups)

    load = pltpu.make_async_copy(w_hbm, w_up, load_sem)
    load.start()
    barrier = pltpu.get_barrier_semaphore()
    for step in range(1, groups):
        pl.semaphore_signal(barrier, inc=1, device_id={"dp": other_group(step)}, device_id_type=pl.DeviceIdType.MESH)
    for step in range(1, shards_of):
        pl.semaphore_signal(barrier, inc=1, device_id={"fsdp": lax.rem(shard + step, shards_of)}, device_id_type=pl.DeviceIdType.MESH)
    pl.semaphore_wait(barrier, groups + shards_of - 2)

    depth = rows // PARTS
    spans = [pl.ds(h * depth, depth) for h in range(PARTS)]
    row_copies = [
        [
            send(
                outgoing.at[other_group(step), span],
                arrived.at[step - 1, span],
                {"dp": other_group(step)},
            )
            for step in range(1, groups)
        ]
        for span in spans
    ]

    right_chip = {"fsdp": lax.rem(chip + 1, chips) * 2 + core}
    left_chip = {"fsdp": lax.rem(chip + chips - 1, chips) * 2 + core}
    beside = {"fsdp": sibling}
    has_right, has_left = chip < chips - 1, chip > 0

    def spread(j, span, device, when=None):
        return send(gathered.at[j, span], gathered.at[j, span], device, when)

    def row_statistics(j):
        values = gathered[j].astype(jnp.float32)
        mean = jnp.sum(values, axis=1, keepdims=True) / width
        means[j] = mean
        squares[j] = jnp.sum((values - mean) * (values - mean), axis=1, keepdims=True)

    def other_core(j):
        return j + 1 - 2 * core

    rightward, leftward, own_beside = [], [], []
    for h, span in enumerate(spans):
        packed = outgoing[group, span].astype(jnp.float32)
        for step in range(1, groups):
            row_copies[h][step - 1].wait_recv()
            packed = packed + arrived[step - 1, span].astype(jnp.float32)
        gathered[shard, span] = packed.astype(jnp.bfloat16)
        rightward.append(spread(shard, span, right_chip, has_right))
        leftward.append(spread(shard, span, left_chip, has_left))
        own_beside.append(spread(shard, span, beside))
    row_statistics(shard)
    waiting = [(None, other_core(shard), own_beside)]

    def take_beside(when, j, copies):
        def take():
            for copy in copies:
                copy.wait_recv()
            row_statistics(j)

        if when is None:
            take()
        else:
            pl.when(when)(take)

    for step in range(1, chips):
        streams = [
            (chip >= step, has_right, right_chip, lax.rem(chip - step + chips, chips), rightward),
            (chip + step < chips, has_left, left_chip, lax.rem(chip + step, chips), leftward),
        ]
        besides = [[], []]
        for h, span in enumerate(spans):
            for side, (here, onward, device, came, stream) in enumerate(streams):
                j = came * 2 + core
                pl.when(here)(stream[h].wait_recv)
                if step < chips - 1:
                    stream[h] = spread(j, span, device, jnp.logical_and(here, onward))
                besides[side].append(spread(j, span, beside, here))
        for entry in waiting:
            take_beside(*entry)
        waiting = []
        for side, (here, onward, device, came, stream) in enumerate(streams):
            j = came * 2 + core
            pl.when(here)(functools.partial(row_statistics, j))
            waiting.append((here, other_core(j), besides[side]))
    for entry in waiting:
        take_beside(*entry)

    mean = means[0]
    for j in range(1, shards_of):
        mean = mean + means[j]
    mean = mean / shards_of
    total = jnp.zeros((rows, 1), jnp.float32)
    for j in range(shards_of):
        offset = means[j] - mean
        total = total + squares[j] + width * (offset * offset)
    inverse = lax.rsqrt(total / full_width + EPS)

    def normalized(j):
        return (gathered[j].astype(jnp.float32) - mean) * inverse

    for j in range(shards_of):
        normed[j] = (normalized(j) * gain[j]).astype(jnp.bfloat16)

    half = pl.ds(pl.multiple_of(core * width, 128), width)
    column_copies = [
        send(normed.at[other_group(step) * 2 + core], columns.at[group, :, half], {"dp": other_group(step)})
        for step in range(1, groups)
    ]
    columns[group, :, :width] = normed[2 * group]
    columns[group, :, width:] = normed[2 * group + 1]

    load.wait()

    def forward(n, carry):
        tile = pl.ds(pl.multiple_of(n * 256, 256), 256)
        acc = jnp.zeros((rows, 256), jnp.float32)
        for j in range(shards_of):
            acc = acc + jnp.dot(
                normed[j], w_up[j * width : (j + 1) * width, tile], preferred_element_type=jnp.float32
            )
        value, slope = gelu_parts(acc + bias[:, tile])
        hidden[:, tile] = value.astype(jnp.bfloat16)
        pieces[group, :, tile] = (grad_hidden[:, tile].astype(jnp.float32) * slope).astype(jnp.bfloat16)
        return carry

    lax.fori_loop(0, hidden_units // 256, forward, 0)
    piece_copies = [
        send(pieces.at[group], pieces.at[group], {"dp": other_group(step)}) for step in range(1, groups)
    ]

    def partial(j):
        lanes = pl.ds(pl.multiple_of(j * width, 128), width)
        return lax.dot_general(
            pieces[group], w_up[lanes, :], (((1,), (1,)), ((), ())), preferred_element_type=jnp.float32
        )

    plain = jnp.zeros((rows, 1), jnp.float32)
    weighted = jnp.zeros((rows, 1), jnp.float32)
    sib_copies, sum_copies = [], {}
    halves = [pl.ds(h * (rows // 2), rows // 2) for h in range(2)]

    def pass_on(i):
        sib_copies[i].wait_recv()
        sum_send[i] = (own[i] + sib_recv[i].astype(jnp.float32)).astype(jnp.bfloat16)
        pass_half(i, 0)
        if i == 0:
            pass_half(i, 1)

    def pass_half(i, h):
        target = lax.rem(chip + 1 + i, chips) * 2 + core
        sum_copies[i, h] = send(
            sum_send.at[i, halves[h]], sum_recv.at[i, halves[h]], {"fsdp": target}
        )

    for i in range(chips):
        base = lax.rem(chip + 1 + i, chips) * 2
        for mine in (False, True):
            j = base + (core if mine else 1 - core)
            part = partial(j)
            scaled = part * gain[j]
            plain = plain + jnp.sum(scaled, axis=1, keepdims=True)
            weighted = weighted + jnp.sum(scaled * normalized(j), axis=1, keepdims=True)
            if mine:
                own[i] = part
            else:
                sib_send[i] = part.astype(jnp.bfloat16)
                sib_copies.append(send(sib_send.at[i], sib_recv.at[i], {"fsdp": sibling}))
        if i > 0:
            pass_on(i - 1)

    for i in range(1, chips - 1):
        pass_half(i, 1)
    lane = lax.broadcasted_iota(jnp.int32, (rows, rows), 1)
    both = jnp.where(lane == 0, plain, jnp.where(lane == 1, weighted, 0.0))
    stats[shard] = both.T[:8]
    stat_copies = [
        send(stats.at[shard], stats.at[shard], {"fsdp": lax.rem(shard + step, shards_of)})
        for step in range(1, shards_of)
    ]
    for step in range(1, groups):
        column_copies[step - 1].wait_recv()
        came = columns.at[source_group(step), :, half]
        column_copies.append(send(came, came, {"fsdp": sibling}))

    for copy in stat_copies:
        copy.wait_recv()
    summed = stats[0]
    for j in range(1, shards_of):
        summed = summed + stats[j]
    upright = jnp.concatenate([summed, jnp.zeros((rows - 8, rows), jnp.float32)], axis=0).T
    plain_mean = upright[:, 0:1] / full_width
    weighted_mean = upright[:, 1:2] / full_width
    sib_copies[chips - 1].wait_recv()
    gain_sum = jnp.zeros((1, width), jnp.float32)
    last = []
    for h, span in enumerate(halves):
        here = slice(h * (rows // 2), (h + 1) * (rows // 2))
        gradient = own[chips - 1, span] + sib_recv[chips - 1, span].astype(jnp.float32)
        for i in range(chips - 1):
            sum_copies[i, h].wait_recv()
            gradient = gradient + sum_recv[i, span].astype(jnp.float32)
        local = (gathered[shard, span].astype(jnp.float32) - mean[here]) * inverse[here]
        back[group, span] = (
            inverse[here] * (gradient * gain[shard] - plain_mean[here] - local * weighted_mean[here])
        ).astype(jnp.bfloat16)
        gain_sum = gain_sum + jnp.sum(gradient * local, axis=0, keepdims=True)
        for step in range(1, groups):
            device = {"dp": other_group(step)}
            last.append(send(back.at[group, span], back.at[group, span], device))
    gain_sums[group] = jnp.broadcast_to(gain_sum, (8, width))
    for step in range(1, groups):
        last.append(send(gain_sums.at[group], gain_sums.at[group], {"dp": other_group(step)}))

    for copy in column_copies[groups - 1 :] + piece_copies:
        copy.wait_recv()

    def weight_rows(n, carry):
        tile = pl.ds(pl.multiple_of(n * 256, 256), 256)
        all_pieces = pieces[...].reshape(groups * rows, hidden_units)
        grad_weight[tile, :] = lax.dot_general(
            columns[:, :, tile].reshape(groups * rows, 256),
            all_pieces,
            (((0,), (0,)), ((), ())),
            preferred_element_type=jnp.float32,
        ).astype(jnp.bfloat16)
        return carry

    lax.fori_loop(0, 2 * width // 256, weight_rows, 0)
    bias_sum = jnp.zeros((1, hidden_units), jnp.float32)
    for j in range(groups):
        bias_sum = bias_sum + jnp.sum(pieces[j].astype(jnp.float32), axis=0, keepdims=True)
    grad_bias[...] = bias_sum
    for copy in last:
        copy.wait_recv()
    for copy, when in pending:
        if when is None:
            copy.wait_send()
        else:
            pl.when(when)(copy.wait_send)


def fused(outgoing, gain, w_up, bias, grad_hidden):
    groups, rows, width = outgoing.shape
    shards_of = lax.axis_size("fsdp")
    hidden_units = bias.shape[0]
    chips = shards_of // 2
    bf16, f32 = jnp.bfloat16, jnp.float32
    copies = (
        (PARTS + 6) * (groups - 1) + PARTS * (4 * chips - 3) + 3 * chips - 2 + shards_of - 1
    )
    vmem = pl.BlockSpec(memory_space=pltpu.VMEM)
    hidden, grad_weight, grad_bias, back, gain_sums = pl.pallas_call(
        functools.partial(fused_kernel, groups, shards_of),
        out_shape=[
            jax.ShapeDtypeStruct((rows, hidden_units), bf16),
            jax.ShapeDtypeStruct((2 * width, hidden_units), bf16),
            jax.ShapeDtypeStruct((1, hidden_units), f32),
            jax.ShapeDtypeStruct((groups, rows, width), bf16),
            jax.ShapeDtypeStruct((groups, 8, width), f32),
        ],
        in_specs=[vmem] * 4 + [pl.BlockSpec(memory_space=pl.ANY)],
        out_specs=[vmem] * 5,
        scratch_shapes=[
            pltpu.VMEM((groups, rows, 2 * width), bf16),
            pltpu.VMEM((groups, rows, hidden_units), bf16),
            pltpu.VMEM(w_up.shape, bf16),
            pltpu.VMEM((groups - 1, rows, width), bf16),
            pltpu.VMEM((shards_of, rows, width), bf16),
            pltpu.VMEM((shards_of, rows, width), bf16),
            pltpu.VMEM((chips, rows, width), bf16),
            pltpu.VMEM((chips, rows, width), bf16),
            pltpu.VMEM((chips, rows, width), f32),
            pltpu.VMEM((chips - 1, rows, width), bf16),
            pltpu.VMEM((chips - 1, rows, width), bf16),
            pltpu.VMEM((shards_of, 8, rows), f32),
            pltpu.VMEM((shards_of, rows, 1), f32),
            pltpu.VMEM((shards_of, rows, 1), f32),
            pltpu.SemaphoreType.DMA((copies,)),
            pltpu.SemaphoreType.DMA((copies,)),
            pltpu.SemaphoreType.DMA,
        ],
        compiler_params=pltpu.CompilerParams(
            collective_id=0, has_side_effects=True, vmem_limit_bytes=50 * 1024 * 1024
        ),
    )(outgoing, gain.reshape(shards_of, 1, width), bias[None], grad_hidden, w_up)
    return (
        hidden,
        grad_weight,
        grad_bias[0],
        back.reshape(groups * rows, width),
        jnp.sum(gain_sums[:, 0], axis=0),
    )


def fits_tiles(groups, shards_of, rows, width, hidden_units):
    return (
        shards_of == 2 * groups and rows == 128 and width % 128 == 0 and hidden_units % 256 == 0
    )


def shards(patches, gain, w_up, bias, grad_hidden, patch_counts, image_source):
    groups, images = patch_counts.shape
    group_rows = grad_hidden.shape[0]
    capacity = patches.shape[0] // images
    local_width = patches.shape[1]
    rows = destination_rows(
        patch_counts, image_source, lax.axis_index("dp"), group_rows, capacity
    )
    numbers = jnp.arange(groups * group_rows, dtype=jnp.int32)
    placed = (rows[None, :] == numbers[:, None]).astype(jnp.bfloat16)
    outgoing = jnp.dot(placed, patches, preferred_element_type=jnp.float32)
    outgoing = outgoing.astype(jnp.bfloat16).reshape(groups, group_rows, local_width)
    tiled = fits_tiles(
        groups, lax.axis_size("fsdp"), group_rows, local_width, grad_hidden.shape[1]
    )
    arrange = fused if tiled else middle
    hidden, grad_weight, grad_bias, gradients, gain_gradient = arrange(
        outgoing, gain, w_up, bias, grad_hidden
    )
    grad_patches = lax.dot_general(
        placed, gradients, (((0,), (0,)), ((), ())), preferred_element_type=jnp.float32
    ).astype(jnp.bfloat16)
    return (hidden, grad_patches, grad_weight, grad_bias, gain_gradient)


def solution(mesh):
    return jax.shard_map(
        shards,
        mesh=mesh,
        in_specs=(P("dp", "fsdp"), P(), P(None, "fsdp"), P("fsdp"), P("dp", "fsdp"), P(), P()),
        out_specs=(P("dp", "fsdp"), P("dp", "fsdp"), P("dp", "fsdp"), P("fsdp"), P("fsdp")),
        check_vma=False,
    )
```

```python
import functools

import jax
import jax.numpy as jnp
from jax import lax
from jax.experimental import pallas as pl
from jax.experimental.pallas import tpu as pltpu
from jax.sharding import PartitionSpec as P

EPS = 1e-06
PARTS = 4
ROOT_HALF = 0.7071067811865476
INV_ROOT_TAU = 0.3989422804014327


def gelu_parts(preact):
    normal_cdf = 0.5 * (1.0 + lax.erf(preact * ROOT_HALF))
    density = jnp.exp(-0.5 * preact * preact) * INV_ROOT_TAU
    return (preact * normal_cdf, normal_cdf + preact * density)


def destination_rows(patch_counts, image_source, group_index, group_rows, capacity):
    groups, images = patch_counts.shape
    numbers = jnp.arange(groups * images, dtype=jnp.int32)[None, :]
    lengths = patch_counts.reshape(1, groups * images)
    mine = lax.dynamic_slice_in_dim(image_source, group_index * images, images, 0)
    image = mine[:, None]
    before = (numbers // images == image // images) & (numbers < image)
    start = jnp.sum(jnp.where(before, lengths, 0), axis=1)
    count = jnp.sum(jnp.where(numbers == image, lengths, 0), axis=1)
    offsets = jnp.arange(capacity, dtype=jnp.int32)
    first = (mine // images) * group_rows + start
    rows = jnp.where(offsets[None, :] < count[:, None], first[:, None] + offsets[None, :], -1)
    return rows.reshape(images * capacity)


def split_in_two(values):
    high = values.astype(jnp.bfloat16)
    low = (values - high.astype(jnp.float32)).astype(jnp.bfloat16)
    return high, low


def weight_gradients(column_rows, piece):
    grad_weight = lax.dot_general(
        column_rows, piece, (((0,), (0,)), ((), ())), preferred_element_type=jnp.float32
    ).astype(jnp.bfloat16)
    return grad_weight, jnp.sum(piece.astype(jnp.float32), axis=0)


def middle(outgoing, gain, w_up, bias, grad_hidden):
    groups, group_rows, local_width = outgoing.shape
    shards_of = lax.axis_size("fsdp")
    arrived = lax.all_to_all(outgoing, "dp", split_axis=0, concat_axis=0, tiled=True)
    packed = jnp.sum(arrived.astype(jnp.float32), axis=0).astype(jnp.bfloat16)
    gathered = lax.all_gather(packed, "fsdp", axis=1, tiled=True)
    full_width = gathered.shape[1]
    values = gathered.astype(jnp.float32)
    row_mean = jnp.mean(values, axis=1, keepdims=True)
    centred_input = values - row_mean
    variance = jnp.mean(centred_input * centred_input, axis=1)
    inverse_deviation = lax.rsqrt(variance + EPS)
    normalized_input = centred_input * inverse_deviation[:, None]
    normed_input = (normalized_input * gain).astype(jnp.bfloat16)
    preact = jnp.dot(normed_input, w_up, preferred_element_type=jnp.float32) + bias
    gelu_value, gelu_slope = gelu_parts(preact)
    hidden = gelu_value.astype(jnp.bfloat16)
    feature_gradient = grad_hidden.astype(jnp.float32) * gelu_slope
    grad_pre = feature_gradient.astype(jnp.bfloat16)
    piece = lax.all_gather(grad_pre, "dp", axis=0, tiled=True)
    column_rows = lax.all_to_all(normed_input, "dp", split_axis=1, concat_axis=0, tiled=True)
    partial = lax.dot_general(
        w_up, grad_pre, (((1,), (1,)), ((), ())), preferred_element_type=jnp.float32
    )
    scaled_partial = partial * gain[:, None]
    sums = jnp.stack(
        [jnp.sum(scaled_partial, axis=0), jnp.sum(scaled_partial * normalized_input.T, axis=0)]
    )
    high, low = split_in_two(sums)
    extra = jnp.concatenate([high, low, jnp.zeros((12, group_rows), jnp.bfloat16)])
    sent = jnp.concatenate(
        [
            partial.astype(jnp.bfloat16).reshape(shards_of, local_width, group_rows),
            jnp.broadcast_to(extra[None], (shards_of,) + extra.shape),
        ],
        axis=1,
    )
    parts = lax.all_to_all(sent, "fsdp", split_axis=0, concat_axis=0, tiled=True)
    total = jnp.sum(parts.astype(jnp.float32), axis=0)
    normed_gradient = total[:local_width]
    row_sums = total[local_width : local_width + 2] + total[local_width + 2 : local_width + 4]
    feature_offset = lax.axis_index("fsdp") * local_width
    own_input = lax.dynamic_slice_in_dim(gathered, feature_offset, local_width, 1)
    normalized_local = (
        (own_input.astype(jnp.float32) - row_mean) * inverse_deviation[:, None]
    ).T
    gain_mine = lax.dynamic_slice_in_dim(gain, feature_offset, local_width, 0)
    packed_gradient = (
        inverse_deviation[None, :]
        * (
            gain_mine[:, None] * normed_gradient
            - row_sums[0][None, :] / full_width
            - normalized_local * row_sums[1][None, :] / full_width
        )
    ).T.astype(jnp.bfloat16)
    high, low = split_in_two(jnp.sum(normed_gradient * normalized_local, axis=1))
    back = jnp.concatenate(
        [packed_gradient, high[None], low[None], jnp.zeros((14, local_width), jnp.bfloat16)]
    )
    all_back = lax.all_gather(back, "dp", axis=0)
    gain_gradient = jnp.sum(
        all_back[:, group_rows : group_rows + 2].astype(jnp.float32), axis=(0, 1)
    )
    gradients = all_back[:, :group_rows].reshape(groups * group_rows, local_width)
    return hidden, *weight_gradients(column_rows, piece), gradients, gain_gradient


def fused_kernel(
    groups, shards_of, outgoing, gain, bias, grad_hidden_hbm, w_hbm,
    hidden, columns, pieces, back, gain_sums,
    grad_hidden, w_up, arrived, gathered, normed, sib_send, sib_recv, own, sum_send, sum_recv, stats, means, squares,
    send_sem, recv_sem, load_sem, small_load_sem,
):
    group, shard = lax.axis_index("dp"), lax.axis_index("fsdp")
    chip, core = shard // 2, lax.rem(shard, 2)
    chips = shards_of // 2
    sibling = shard + 1 - 2 * core
    rows, width = outgoing.shape[1:]
    full_width = shards_of * width
    hidden_units = bias.shape[1]
    counter = [0]
    pending = []

    def send(source, target, device, when=None):
        index = counter[0]
        counter[0] += 1
        copy = pltpu.make_async_remote_copy(
            src_ref=source,
            dst_ref=target,
            send_sem=send_sem.at[index],
            recv_sem=recv_sem.at[index],
            device_id=device,
            device_id_type=pl.DeviceIdType.MESH,
        )
        if when is None:
            copy.start()
        else:
            pl.when(when)(copy.start)
        pending.append((copy, when))
        return copy

    def other_group(step):
        return lax.rem(group + step, groups)

    def source_group(step):
        return lax.rem(group - step + groups, groups)

    load = pltpu.make_async_copy(w_hbm, w_up, load_sem)
    load.start()
    small_load = pltpu.make_async_copy(grad_hidden_hbm, grad_hidden, small_load_sem)
    small_load.start()
    barrier = pltpu.get_barrier_semaphore()
    for step in range(1, groups):
        pl.semaphore_signal(barrier, inc=1, device_id={"dp": other_group(step)}, device_id_type=pl.DeviceIdType.MESH)
    for step in range(1, shards_of):
        pl.semaphore_signal(barrier, inc=1, device_id={"fsdp": lax.rem(shard + step, shards_of)}, device_id_type=pl.DeviceIdType.MESH)
    pl.semaphore_wait(barrier, groups + shards_of - 2)

    depth = rows // PARTS
    spans = [pl.ds(h * depth, depth) for h in range(PARTS)]
    row_copies = [
        [
            send(
                outgoing.at[other_group(step), span],
                arrived.at[step - 1, span],
                {"dp": other_group(step)},
            )
            for step in range(1, groups)
        ]
        for span in spans
    ]

    right_chip = {"fsdp": lax.rem(chip + 1, chips) * 2 + core}
    left_chip = {"fsdp": lax.rem(chip + chips - 1, chips) * 2 + core}
    beside = {"fsdp": sibling}
    has_right, has_left = chip < chips - 1, chip > 0

    def spread(j, span, device, when=None):
        return send(gathered.at[j, span], gathered.at[j, span], device, when)

    def row_statistics(j):
        values = gathered[j].astype(jnp.float32)
        mean = jnp.sum(values, axis=1, keepdims=True) / width
        means[j] = mean
        squares[j] = jnp.sum((values - mean) * (values - mean), axis=1, keepdims=True)

    def other_core(j):
        return j + 1 - 2 * core

    rightward, leftward, own_beside = [], [], []
    for h, span in enumerate(spans):
        packed = outgoing[group, span].astype(jnp.float32)
        for step in range(1, groups):
            row_copies[h][step - 1].wait_recv()
            packed = packed + arrived[step - 1, span].astype(jnp.float32)
        gathered[shard, span] = packed.astype(jnp.bfloat16)
        rightward.append(spread(shard, span, right_chip, has_right))
        leftward.append(spread(shard, span, left_chip, has_left))
        own_beside.append(spread(shard, span, beside))
    row_statistics(shard)
    waiting = [(None, other_core(shard), own_beside)]

    def take_beside(when, j, copies):
        def take():
            for copy in copies:
                copy.wait_recv()
            row_statistics(j)

        if when is None:
            take()
        else:
            pl.when(when)(take)

    for step in range(1, chips):
        streams = [
            (chip >= step, has_right, right_chip, lax.rem(chip - step + chips, chips), rightward),
            (chip + step < chips, has_left, left_chip, lax.rem(chip + step, chips), leftward),
        ]
        besides = [[], []]
        for h, span in enumerate(spans):
            for side, (here, onward, device, came, stream) in enumerate(streams):
                j = came * 2 + core
                pl.when(here)(stream[h].wait_recv)
                if step < chips - 1:
                    stream[h] = spread(j, span, device, jnp.logical_and(here, onward))
                besides[side].append(spread(j, span, beside, here))
        for entry in waiting:
            take_beside(*entry)
        waiting = []
        for side, (here, onward, device, came, stream) in enumerate(streams):
            j = came * 2 + core
            pl.when(here)(functools.partial(row_statistics, j))
            waiting.append((here, other_core(j), besides[side]))
    for entry in waiting:
        take_beside(*entry)

    mean = means[0]
    for j in range(1, shards_of):
        mean = mean + means[j]
    mean = mean / shards_of
    total = jnp.zeros((rows, 1), jnp.float32)
    for j in range(shards_of):
        offset = means[j] - mean
        total = total + squares[j] + width * (offset * offset)
    inverse = lax.rsqrt(total / full_width + EPS)

    def normalized(j):
        return (gathered[j].astype(jnp.float32) - mean) * inverse

    for j in range(shards_of):
        normed[j] = (normalized(j) * gain[j]).astype(jnp.bfloat16)

    half = pl.ds(pl.multiple_of(core * width, 128), width)
    column_copies = [
        send(normed.at[other_group(step) * 2 + core], columns.at[group, :, half], {"dp": other_group(step)})
        for step in range(1, groups)
    ]
    columns[group, :, :width] = normed[2 * group]
    columns[group, :, width:] = normed[2 * group + 1]

    load.wait()
    small_load.wait()

    def forward(n, carry):
        tile = pl.ds(pl.multiple_of(n * 256, 256), 256)
        acc = jnp.zeros((rows, 256), jnp.float32)
        for j in range(shards_of):
            acc = acc + jnp.dot(
                normed[j], w_up[j * width : (j + 1) * width, tile], preferred_element_type=jnp.float32
            )
        value, slope = gelu_parts(acc + bias[:, tile])
        hidden[:, tile] = value.astype(jnp.bfloat16)
        pieces[group, :, tile] = (grad_hidden[:, tile].astype(jnp.float32) * slope).astype(jnp.bfloat16)
        return carry

    lax.fori_loop(0, hidden_units // 256, forward, 0)
    piece_copies = [
        send(pieces.at[group], pieces.at[group], {"dp": other_group(step)}) for step in range(1, groups)
    ]

    def partial(j):
        lanes = pl.ds(pl.multiple_of(j * width, 128), width)
        return lax.dot_general(
            pieces[group], w_up[lanes, :], (((1,), (1,)), ((), ())), preferred_element_type=jnp.float32
        )

    plain = jnp.zeros((rows, 1), jnp.float32)
    weighted = jnp.zeros((rows, 1), jnp.float32)
    sib_copies, sum_copies = [], {}
    halves = [pl.ds(h * (rows // 2), rows // 2) for h in range(2)]

    def pass_on(i):
        sib_copies[i].wait_recv()
        sum_send[i] = (own[i] + sib_recv[i].astype(jnp.float32)).astype(jnp.bfloat16)
        pass_half(i, 0)
        if i == 0:
            pass_half(i, 1)

    def pass_half(i, h):
        target = lax.rem(chip + 1 + i, chips) * 2 + core
        sum_copies[i, h] = send(
            sum_send.at[i, halves[h]], sum_recv.at[i, halves[h]], {"fsdp": target}
        )

    for i in range(chips):
        base = lax.rem(chip + 1 + i, chips) * 2
        for mine in (False, True):
            j = base + (core if mine else 1 - core)
            part = partial(j)
            scaled = part * gain[j]
            plain = plain + jnp.sum(scaled, axis=1, keepdims=True)
            weighted = weighted + jnp.sum(scaled * normalized(j), axis=1, keepdims=True)
            if mine:
                own[i] = part
            else:
                sib_send[i] = part.astype(jnp.bfloat16)
                sib_copies.append(send(sib_send.at[i], sib_recv.at[i], {"fsdp": sibling}))
        if i > 0:
            pass_on(i - 1)

    for i in range(1, chips - 1):
        pass_half(i, 1)
    lane = lax.broadcasted_iota(jnp.int32, (rows, rows), 1)
    both = jnp.where(lane == 0, plain, jnp.where(lane == 1, weighted, 0.0))
    stats[shard] = both.T[:8]
    stat_copies = [
        send(stats.at[shard], stats.at[shard], {"fsdp": lax.rem(shard + step, shards_of)})
        for step in range(1, shards_of)
    ]
    for step in range(1, groups):
        column_copies[step - 1].wait_recv()
        came = columns.at[source_group(step), :, half]
        column_copies.append(send(came, came, {"fsdp": sibling}))

    for copy in stat_copies:
        copy.wait_recv()
    summed = stats[0]
    for j in range(1, shards_of):
        summed = summed + stats[j]
    upright = jnp.concatenate([summed, jnp.zeros((rows - 8, rows), jnp.float32)], axis=0).T
    plain_mean = upright[:, 0:1] / full_width
    weighted_mean = upright[:, 1:2] / full_width
    sib_copies[chips - 1].wait_recv()
    gain_sum = jnp.zeros((1, width), jnp.float32)
    last = []
    for h, span in enumerate(halves):
        here = slice(h * (rows // 2), (h + 1) * (rows // 2))
        gradient = own[chips - 1, span] + sib_recv[chips - 1, span].astype(jnp.float32)
        for i in range(chips - 1):
            sum_copies[i, h].wait_recv()
            gradient = gradient + sum_recv[i, span].astype(jnp.float32)
        local = (gathered[shard, span].astype(jnp.float32) - mean[here]) * inverse[here]
        back[group, span] = (
            inverse[here] * (gradient * gain[shard] - plain_mean[here] - local * weighted_mean[here])
        ).astype(jnp.bfloat16)
        gain_sum = gain_sum + jnp.sum(gradient * local, axis=0, keepdims=True)
        for step in range(1, groups):
            device = {"dp": other_group(step)}
            last.append(send(back.at[group, span], back.at[group, span], device))
    gain_sums[group] = jnp.broadcast_to(gain_sum, (8, width))
    for step in range(1, groups):
        last.append(send(gain_sums.at[group], gain_sums.at[group], {"dp": other_group(step)}))

    for copy in column_copies[groups - 1 :] + piece_copies:
        copy.wait_recv()

    for copy in last:
        copy.wait_recv()
    for copy, when in pending:
        if when is None:
            copy.wait_send()
        else:
            pl.when(when)(copy.wait_send)


def fused(outgoing, gain, w_up, bias, grad_hidden):
    groups, rows, width = outgoing.shape
    shards_of = lax.axis_size("fsdp")
    hidden_units = bias.shape[0]
    chips = shards_of // 2
    bf16, f32 = jnp.bfloat16, jnp.float32
    copies = (
        (PARTS + 6) * (groups - 1) + PARTS * (4 * chips - 3) + 3 * chips - 2 + shards_of - 1
    )
    vmem = pl.BlockSpec(memory_space=pltpu.VMEM)
    hidden, columns, pieces, back, gain_sums = pl.pallas_call(
        functools.partial(fused_kernel, groups, shards_of),
        out_shape=[
            jax.ShapeDtypeStruct((rows, hidden_units), bf16),
            jax.ShapeDtypeStruct((groups, rows, 2 * width), bf16),
            jax.ShapeDtypeStruct((groups, rows, hidden_units), bf16),
            jax.ShapeDtypeStruct((groups, rows, width), bf16),
            jax.ShapeDtypeStruct((groups, 8, width), f32),
        ],
        in_specs=[vmem] * 3 + [pl.BlockSpec(memory_space=pl.ANY)] * 2,
        out_specs=[vmem] * 5,
        scratch_shapes=[
            pltpu.VMEM((rows, hidden_units), bf16),
            pltpu.VMEM(w_up.shape, bf16),
            pltpu.VMEM((groups - 1, rows, width), bf16),
            pltpu.VMEM((shards_of, rows, width), bf16),
            pltpu.VMEM((shards_of, rows, width), bf16),
            pltpu.VMEM((chips, rows, width), bf16),
            pltpu.VMEM((chips, rows, width), bf16),
            pltpu.VMEM((chips, rows, width), f32),
            pltpu.VMEM((chips - 1, rows, width), bf16),
            pltpu.VMEM((chips - 1, rows, width), bf16),
            pltpu.VMEM((shards_of, 8, rows), f32),
            pltpu.VMEM((shards_of, rows, 1), f32),
            pltpu.VMEM((shards_of, rows, 1), f32),
            pltpu.SemaphoreType.DMA((copies,)),
            pltpu.SemaphoreType.DMA((copies,)),
            pltpu.SemaphoreType.DMA,
            pltpu.SemaphoreType.DMA,
        ],
        compiler_params=pltpu.CompilerParams(
            collective_id=0, has_side_effects=True, vmem_limit_bytes=50 * 1024 * 1024
        ),
    )(outgoing, gain.reshape(shards_of, 1, width), bias[None], grad_hidden, w_up)
    return (
        hidden,
        *weight_gradients(
            columns.reshape(groups * rows, 2 * width), pieces.reshape(groups * rows, hidden_units)
        ),
        back.reshape(groups * rows, width),
        jnp.sum(gain_sums[:, 0], axis=0),
    )


def fits_tiles(groups, shards_of, rows, width, hidden_units):
    return (
        shards_of == 2 * groups and rows == 128 and width % 128 == 0 and hidden_units % 256 == 0
    )


def shards(patches, gain, w_up, bias, grad_hidden, patch_counts, image_source):
    groups, images = patch_counts.shape
    group_rows = grad_hidden.shape[0]
    capacity = patches.shape[0] // images
    local_width = patches.shape[1]
    rows = destination_rows(
        patch_counts, image_source, lax.axis_index("dp"), group_rows, capacity
    )
    numbers = jnp.arange(groups * group_rows, dtype=jnp.int32)
    placed = (rows[None, :] == numbers[:, None]).astype(jnp.bfloat16)
    outgoing = jnp.dot(placed, patches, preferred_element_type=jnp.float32)
    outgoing = outgoing.astype(jnp.bfloat16).reshape(groups, group_rows, local_width)
    tiled = fits_tiles(
        groups, lax.axis_size("fsdp"), group_rows, local_width, grad_hidden.shape[1]
    )
    arrange = fused if tiled else middle
    hidden, grad_weight, grad_bias, gradients, gain_gradient = arrange(
        outgoing, gain, w_up, bias, grad_hidden
    )
    grad_patches = lax.dot_general(
        placed, gradients, (((0,), (0,)), ((), ())), preferred_element_type=jnp.float32
    ).astype(jnp.bfloat16)
    return (hidden, grad_patches, grad_weight, grad_bias, gain_gradient)


def solution(mesh):
    return jax.shard_map(
        shards,
        mesh=mesh,
        in_specs=(P("dp", "fsdp"), P(), P(None, "fsdp"), P("fsdp"), P("dp", "fsdp"), P(), P()),
        out_specs=(P("dp", "fsdp"), P("dp", "fsdp"), P("dp", "fsdp"), P("fsdp"), P("fsdp")),
        check_vma=False,
    )
```
